256 devices in a mesh: mode: 64 (over z, y, core), blk: 4 (over x).
Axes of the slice: x: 4, y: 4, z: 8, core: 2. Of those that a mesh axis runs over, the one named last changes fastest.
Arguments:
- emissive: bfloat16 [512, 3072, 128], P('mode', 'blk'), may hold values from 0.099609375 to 3
- classes: int32 [3072], P('blk'), may hold values from 0 to 7
- emissivity: float32 [8, 8], replicated, may hold values from 0.1 to 0.9
- mode_ids: int32 [64], replicated, may hold values from 0 to 256, as said below
- view_factor: bfloat16 [64, 2, 3072, 3072], P('mode', None, 'blk'), may hold values from -0.3125 to 0.3125
Outputs:
- radiosity: bfloat16 [512, 3072, 128], P('mode', 'blk')
The draws below stay inside these ranges and needn't reach their ends.
Inputs may be any that keep to these rules, and one draw needn't show every extreme that they name: `mode_ids`: 64 different azimuthal mode numbers; 0 and 256 are always among them.
All inputs are finite; a program needn't handle non-finite values.
Results may differ from the reference program's by a relative error of at most 0.008.
Values may be sent and summed in bfloat16 or wider, within the bound.
A program may use at most 64 MiB of HBM per device.

```python
import math
import jax
import jax.numpy as jnp
from jax import lax

A = 512
P_SIZE = 3072
B = 8
NCLASS = 8
KM = 64
C = 128


def draw_mode_ids(key, part):
    key = jax.random.fold_in(key, 11)
    inner = jax.random.permutation(key, A // 2 - 1)[:KM - 2] + 1
    chosen = jnp.concatenate([jnp.array([0, A // 2], dtype=jnp.int32), inner.astype(jnp.int32)])
    order = jax.random.permutation(jax.random.fold_in(key, 1), KM)
    return chosen[order].astype(jnp.int32)


def touch_ends(values, stream_key, low, high):
    dims = values.shape
    place = [jax.random.randint(jax.random.fold_in(stream_key, axis), (), 0, dims[axis]) for axis in range(len(dims))]
    values = values.at[tuple(place)].set(low)
    longest = dims.index(max(dims))
    place[longest] = (place[longest] + 1) % dims[longest]
    return values.at[tuple(place)].set(high)


def shard_levels(key, dims, cuts, low, largest):
    loudness = 1.0
    for axis_at, blocks in cuts:
        heights = jax.random.uniform(jax.random.fold_in(jax.random.fold_in(key, 6), axis_at), (blocks,), jnp.float32, low / len(cuts), largest / len(cuts))
        loudness = loudness * jnp.repeat(jnp.exp(heights), dims[axis_at] // blocks).reshape((-1,) + (1,) * (len(dims) - 1 - axis_at))
    return loudness


def noise(stream_key, shape, spread, limit, shards=(), kind=jnp.bfloat16):
    result = jax.random.normal(stream_key, shape, jnp.float32) * spread
    if len(shards) > 0:
        result = shard_levels(stream_key, shape, shards, -0.22, 0.18) * result
    return jnp.clip(result, min=-limit, max=limit).astype(kind)


def setup_inputs(seed: int = 0) -> dict:
    key_list = jax.random.split(jax.random.key(seed), 6)
    emissive = jnp.clip(jnp.exp(math.log(3.0) - 3.4051113 * jax.random.uniform(key_list[0], (A, P_SIZE, C), jnp.float32) ** shard_levels(key_list[0], (A, P_SIZE, C), ((0, 64), (1, 4)), -0.2, 0.2)), 0.099609375, 3.0).astype(jnp.bfloat16)
    classes = touch_ends(jax.random.randint(key_list[1], (P_SIZE,), 0, NCLASS), jax.random.fold_in(key_list[1], 1), 0, NCLASS - 1).astype(jnp.int32)
    emissivity = jnp.clip(jax.random.uniform(key_list[2], (NCLASS, B), jnp.float32, 0.1, 0.9), 0.1, 0.9)
    mode_ids = draw_mode_ids(jax.random.fold_in(key_list[5], 71), 0)
    view_factor = noise(key_list[4], (KM, 2, P_SIZE, P_SIZE), (P_SIZE // 8) ** -0.5, 0.3125, ((0, 64), (2, 4)))
    return {"emissive": emissive, "classes": classes, "emissivity": emissivity, "mode_ids": mode_ids, "view_factor": view_factor}


def tables(mode_ids):
    mode_count = mode_ids.shape[0]
    stations = jnp.arange(A, dtype=jnp.int32)
    twists = (mode_ids[:, None] * stations[None, :]) % A
    phases = twists.astype(jnp.float32) * (2.0 * math.pi / A)
    cosine = jnp.cos(phases)
    sine_part = jnp.sin(phases)
    forward = jnp.stack([cosine, -sine_part], axis=1).reshape(2 * mode_count, A).astype(jnp.bfloat16)
    real_only = (mode_ids == 0) | (mode_ids == A // 2)
    weight = jnp.where(real_only, 1.0 / A, 2.0 / A).astype(jnp.float32)[:, None]
    inverse = jnp.stack([weight * cosine, -weight * sine_part], axis=1).reshape(2 * mode_count, A).astype(jnp.bfloat16)
    return forward, inverse


def matmul(left, right):
    return jnp.dot(left, right, precision=lax.Precision.HIGHEST)


def reference(emissive, classes, emissivity, mode_ids, view_factor):
    band_of = jnp.arange(C, dtype=jnp.int32) % B
    emission = emissivity[classes][:, band_of]
    emitted = (emission[None] * emissive.astype(jnp.float32)).astype(jnp.bfloat16)
    forward, inverse = tables(mode_ids)
    spectrum = jnp.dot(forward, emitted.reshape(A, P_SIZE * C), preferred_element_type=jnp.float32)
    spectrum = spectrum.astype(jnp.bfloat16).reshape(KM, 2, P_SIZE, C)

    def reflect(pair):
        factors, modal_rows = pair
        factors = factors.astype(jnp.float32)
        modal_rows = modal_rows.astype(jnp.float32)
        real_part = matmul(factors[0], modal_rows[0]) - matmul(factors[1], modal_rows[1])
        imag_part = matmul(factors[0], modal_rows[1]) + matmul(factors[1], modal_rows[0])
        return jnp.stack([real_part, imag_part]).astype(jnp.bfloat16)

    reflected = lax.map(reflect, (view_factor, spectrum))
    irradiance = jnp.dot(inverse.T, reflected.reshape(2 * KM, P_SIZE * C), preferred_element_type=jnp.float32)
    irradiance = irradiance.astype(jnp.bfloat16).reshape(A, P_SIZE, C)
    radiosity = emitted.astype(jnp.float32) + (1.0 - emission)[None] * irradiance.astype(jnp.float32)
    return radiosity.astype(jnp.bfloat16)
```

```python
import functools
import math

import jax
import jax.numpy as jnp
from jax import lax
from jax.experimental import pallas as pl
from jax.experimental.pallas import tpu as pltpu
from jax.sharding import PartitionSpec as P

A = 512
Z, Y, CORES, X = 8, 4, 2, 4
Q = Y * CORES
S = A // (Z * Q)
SZ = S * Q
T = 16
NC = 3
PATCHES = 768
PC = PATCHES // NC
W = PC // Q
G = W // T
C = 128
R = 2 * Q
RT = R * T
MESH = pl.DeviceIdType.MESH
F32, BF16 = jnp.float32, jnp.bfloat16


def tables(mode_ids, stations):
    twists = mode_ids[:, None] * stations[None, :] % A
    phases = twists.astype(F32) * (2.0 * math.pi / A)
    cosine, sine = jnp.cos(phases), jnp.sin(phases)
    rows = 2 * mode_ids.shape[0]
    forward = jnp.stack([cosine, -sine], axis=1).reshape(rows, -1)
    real_only = (mode_ids == 0) | (mode_ids == A // 2)
    weight = jnp.where(real_only, 1.0 / A, 2.0 / A).astype(F32)[:, None]
    inverse = jnp.stack([weight * cosine, -weight * sine], axis=1).reshape(rows, -1)
    return forward, inverse


def spread(table_ref, out_ref):
    rows, width = table_ref.shape
    mask = lax.broadcasted_iota(jnp.int32, (T, width), 0) == (
        lax.broadcasted_iota(jnp.int32, (T, width), 1) % T
    )

    def body(b, _):
        block = table_ref[pl.ds(pl.multiple_of(b * 8, 8), 8), :]
        for i in range(8):
            row = jnp.broadcast_to(block[i : i + 1, :], (T, width))
            at = pl.multiple_of((b * 8 + i) * T, T)
            out_ref[pl.ds(at, T), :] = jnp.where(mask, row, 0.0).astype(BF16)
        return 0

    lax.fori_loop(0, rows // 8, body, 0)


def kernel(
    emissive, emission, ftab, itab, factor_hbm, out,
    fk, ik, factor, emitted, station, rs_out, rs_in, spec, xs, acc, refl, gath, irr_out, irr,
    f_sem, a_send, a_recv, rs_send, rs_recv, c_send, c_recv, x_send, x_recv,
    d_send, d_recv, g_send, g_recv, h_send, h_recv,
):
    me, x = lax.axis_index("mode"), lax.axis_index("blk")
    z, q = me // Q, me % Q
    y, core = q // CORES, q % CORES

    def at_q(other):
        return {"mode": z * Q + other, "blk": x}

    def at_z(step):
        return {"mode": ((z + step + Z) % Z) * Q + q, "blk": x}

    def at_x(step):
        return {"mode": me, "blk": (x + step + X) % X}

    def copy(src, dst, send, recv, device):
        return pltpu.make_async_remote_copy(
            src_ref=src, dst_ref=dst, send_sem=send, recv_sem=recv,
            device_id=device, device_id_type=MESH,
        )

    sent = []

    def send(src, dst, s, r, device):
        op = copy(src, dst, s, r, device)
        op.start()
        sent.append(op)

    def arrived(dst, s, r):
        copy(dst, dst, s, r, at_z(1)).wait_recv()

    load = pltpu.make_async_copy(factor_hbm, factor, f_sem)
    load.start()

    barrier = pltpu.get_barrier_semaphore()
    peers = [at_q((q + k) % Q) for k in range(1, Q)]
    peers += [at_z(1), at_z(-1), at_x(1), at_x(-1)]
    for device in peers:
        pl.semaphore_signal(barrier, inc=1, device_id=device, device_id_type=MESH)

    def rows_of(c, other):
        return pl.ds(pl.multiple_of(c * PC + other * W, T), W)

    def emit(c):
        rows = pl.ds(c * PC, PC)
        share = emission[rows, :]

        def body(s, _):
            emitted[s, rows, :] = (share * emissive[s, rows, :].astype(F32)).astype(BF16)
            return 0

        lax.fori_loop(0, S, body, 0)

    def stations_out(c):
        for k in range(1, Q):
            other = (q + k) % Q
            send(
                emitted.at[:, rows_of(c, other), :], station.at[c, pl.ds(q * S, S)],
                a_send.at[c, k], a_recv.at[c, k], at_q(other),
            )
        station[c, pl.ds(q * S, S)] = emitted[:, rows_of(c, q), :]

    def stations_in(c):
        for k in range(1, Q):
            other = (q - k + Q) % Q
            arrived(station.at[c, pl.ds(other * S, S)], a_send.at[c, k], a_recv.at[c, k])

    def partial(c, target):
        parts = [station[c, :, g * T : (g + 1) * T, :].reshape(SZ * T, C) for g in range(G)]
        right = parts[0] if G == 1 else jnp.concatenate(parts, axis=1)
        left = fk[pl.ds(pl.multiple_of(target * RT, RT), RT), :]
        return jnp.dot(left, right, preferred_element_type=F32)

    def piece(value, g):
        return value[:, g * C : (g + 1) * C].reshape(R, T, C)

    def rs_step(c, t):
        half = R // 2
        if t == 0:
            stations_in(c)
            value = partial(c, (z + 4) % Z)
            for way in range(2):
                rows = slice(way * half, (way + 1) * half)
                for g in range(G):
                    rs_out[way, c, 0, rows, g * T : (g + 1) * T, :] = piece(value, g)[rows].astype(BF16)
                where = pl.ds(way * half, half)
                send(
                    rs_out.at[way, c, 0, where], rs_in.at[way, c, 0, where],
                    rs_send.at[way, c, 0], rs_recv.at[way, c, 0], at_z(1 - 2 * way),
                )
            return
        for way in range(2):
            target = (z + 4 - t) % Z if way == 0 else (z + 4 + t) % Z
            value = partial(c, target)
            if t == 1:
                where = pl.ds(way * half, half)
                arrived(rs_in.at[way, c, 0, where], rs_send.at[way, c, 0], rs_recv.at[way, c, 0])
            else:
                arrived(rs_in.at[way, c, t - 1], rs_send.at[way, c, t - 1], rs_recv.at[way, c, t - 1])
            for g in range(G):
                cols = slice(g * T, (g + 1) * T)
                mine = piece(value, g)
                if t == 1:
                    hit = slice(way * half, (way + 1) * half)
                    miss = slice((1 - way) * half, (2 - way) * half)
                    total = mine[hit] + rs_in[way, c, 0, hit, cols, :].astype(F32)
                    rs_out[way, c, t, hit, cols, :] = total.astype(BF16)
                    rs_out[way, c, t, miss, cols, :] = mine[miss].astype(BF16)
                else:
                    total = mine + rs_in[way, c, t - 1, :, cols, :].astype(F32)
                    rs_out[way, c, t, :, cols, :] = total.astype(BF16)
            send(
                rs_out.at[way, c, t], rs_in.at[way, c, t],
                rs_send.at[way, c, t], rs_recv.at[way, c, t], at_z(1 - 2 * way),
            )

    def rs_final(c):
        value = partial(c, z)
        for way in range(2):
            arrived(rs_in.at[way, c, 3], rs_send.at[way, c, 3], rs_recv.at[way, c, 3])
        for g in range(G):
            cols = slice(g * T, (g + 1) * T)
            total = piece(value, g) + (
                rs_in[0, c, 3, :, cols, :].astype(F32) + rs_in[1, c, 3, :, cols, :].astype(F32)
            )
            spec[c, :, cols, :] = total.astype(BF16)
        for k in range(1, Q):
            other = (q + k) % Q
            send(
                spec.at[c, pl.ds(other * 2, 2)], xs.at[x, :, rows_of(c, q), :],
                c_send.at[c, k], c_recv.at[c, k], at_q(other),
            )
        xs[x, :, rows_of(c, q), :] = spec[c, pl.ds(q * 2, 2)]

    def gather_first(c):
        for k in range(1, Q):
            other = (q - k + Q) % Q
            arrived(xs.at[x, :, rows_of(c, other), :], c_send.at[c, k], c_recv.at[c, k])
        rows = pl.ds(c * PC, PC)
        for way in range(2):
            send(
                xs.at[x, :, rows, :], xs.at[x, :, rows, :],
                x_send.at[0, way, c], x_recv.at[0, way, c], at_x(1 - 2 * way),
            )

    def reflect(c, source):
        rows = pl.ds(c * PC, PC)
        real, imag = xs[source, 0, rows, :], xs[source, 1, rows, :]
        right = jnp.concatenate(
            [jnp.concatenate([real, imag], axis=1), jnp.concatenate([-imag, real], axis=1)], axis=0
        )
        at = pl.ds(pl.multiple_of(source * PATCHES + c * PC, PC), PC)

        def body(b, _):
            to = pl.ds(pl.multiple_of(b * 256, 256), 256)
            left = jnp.concatenate([factor[0, to, at], factor[1, to, at]], axis=1)
            acc[to, :] += jnp.dot(left, right, preferred_element_type=F32)
            return 0

        lax.fori_loop(0, PATCHES // 256, body, 0)

    def gather_second(c):
        rows = pl.ds(c * PC, PC)
        reflect(c, x)
        for way in range(2):
            source = (x + X - 1 + 2 * way) % X
            arrived(xs.at[source, :, rows, :], x_send.at[0, way, c], x_recv.at[0, way, c])
            send(
                xs.at[source, way, rows, :], xs.at[source, way, rows, :],
                x_send.at[1, way, c], x_recv.at[1, way, c], at_x(1 - 2 * way),
            )
        for way in range(2):
            reflect(c, (x + X - 1 + 2 * way) % X)

    def gather_third(c):
        rows = pl.ds(c * PC, PC)
        source = (x + 2) % X
        for way in range(2):
            arrived(xs.at[source, way, rows, :], x_send.at[1, way, c], x_recv.at[1, way, c])
        reflect(c, source)

    def reflected_out(c):
        rows = pl.ds(c * PC, PC)
        for part in range(2):
            refl[part, rows, :] = acc[rows, part * C : (part + 1) * C].astype(BF16)
        for k in range(1, Q):
            other = (q + k) % Q
            send(
                refl.at[:, rows_of(c, other), :], gath.at[c, z, pl.ds(q * 2, 2)],
                d_send.at[c, k], d_recv.at[c, k], at_q(other),
            )
        gath[c, z, pl.ds(q * 2, 2)] = refl[:, rows_of(c, q), :]

    def ag_step(c, t):
        half = R // 2
        if t == 0:
            for k in range(1, Q):
                other = (q - k + Q) % Q
                arrived(gath.at[c, z, pl.ds(other * 2, 2)], d_send.at[c, k], d_recv.at[c, k])
        for way in range(2):
            source = (z - t + Z) % Z if way == 0 else (z + t) % Z
            if t > 0:
                arrived(gath.at[c, source], g_send.at[way, c, t - 1], g_recv.at[way, c, t - 1])
            block = gath.at[c, source]
            if t == 3:
                block = gath.at[c, source, pl.ds(way * half, half)]
            send(block, block, g_send.at[way, c, t], g_recv.at[way, c, t], at_z(1 - 2 * way))

    def irradiance_out(c):
        half = R // 2
        far = (z + 4) % Z
        for way in range(2):
            arrived(
                gath.at[c, far, pl.ds(way * half, half)], g_send.at[way, c, 3], g_recv.at[way, c, 3]
            )
        parts = [gath[c, :, :, g * T : (g + 1) * T, :].reshape(Z * RT, C) for g in range(G)]
        right = parts[0] if G == 1 else jnp.concatenate(parts, axis=1)
        rows = 2 * S * T
        for k in range(Y):
            other = (y + k) % Y
            left = ik[pl.ds(pl.multiple_of(other * rows, rows), rows), :]
            value = jnp.dot(left, right, preferred_element_type=F32)
            for g in range(G):
                irr_out[c, pl.ds(other * 2 * S, 2 * S), g * T : (g + 1) * T, :] = (
                    value[:, g * C : (g + 1) * C].reshape(2 * S, T, C).astype(BF16)
                )
            for j in range(CORES):
                if k == 0 and j == 0:
                    continue
                to = other * CORES + (core + j) % CORES
                n = k * CORES + j
                send(
                    irr_out.at[c, pl.ds(to * S, S)], irr.at[:, rows_of(c, q), :],
                    h_send.at[c, n], h_recv.at[c, n], at_q(to),
                )
        irr[:, rows_of(c, q), :] = irr_out[c, pl.ds(q * S, S)]

    def finish(c):
        for k in range(Y):
            for j in range(CORES):
                if k == 0 and j == 0:
                    continue
                source = ((y - k + Y) % Y) * CORES + (core + j) % CORES
                n = k * CORES + j
                arrived(irr.at[:, rows_of(c, source), :], h_send.at[c, n], h_recv.at[c, n])
        rows = pl.ds(c * PC, PC)
        rest = 1.0 - emission[rows, :]

        def body(s, _):
            total = emitted[s, rows, :].astype(F32) + rest * irr[s, rows, :].astype(F32)
            out[s, rows, :] = total.astype(BF16)
            return 0

        lax.fori_loop(0, S, body, 0)

    emit(0)
    pl.semaphore_wait(barrier, len(peers))
    stations_out(0)
    for c in range(1, NC):
        emit(c)
        stations_out(c)
    spread(ftab, fk)
    spread(itab, ik)
    acc[...] = jnp.zeros_like(acc)

    stages = [functools.partial(rs_step, t=t) for t in range(4)]
    stages += [rs_final, gather_first, gather_second, gather_third]
    loaded = False
    for slot in range(len(stages) + NC - 1):
        for c in range(NC):
            stage = slot - c
            if 0 <= stage < len(stages):
                if stages[stage] is gather_second and not loaded:
                    load.wait()
                    loaded = True
                stages[stage](c)
    for c in range(NC):
        reflected_out(c)
    for t in range(4):
        for c in range(NC):
            ag_step(c, t)
    for c in range(NC):
        irradiance_out(c)
    for c in range(NC):
        finish(c)
    for op in sent:
        op.wait_send()


def local(emissive, classes, emissivity, mode_ids, view_factor):
    pick = classes[:, None] == jnp.arange(emissivity.shape[0], dtype=jnp.int32)[None, :]
    rates = jnp.tile(emissivity, (1, C // emissivity.shape[1]))
    emission = jnp.sum(jnp.where(pick[:, :, None], rates[None], 0.0), axis=1)
    z = lax.axis_index("mode") // Q
    forward, inverse = tables(mode_ids, z * SZ + jnp.arange(SZ, dtype=jnp.int32))
    ftab = jnp.repeat(forward, T, axis=1)
    itab = jnp.repeat(inverse.T, T, axis=1)
    vmem = pl.BlockSpec(memory_space=pltpu.VMEM)
    dma = pltpu.SemaphoreType.DMA
    return pl.pallas_call(
        kernel,
        out_shape=jax.ShapeDtypeStruct(emissive.shape, BF16),
        in_specs=[vmem] * 4 + [pl.BlockSpec(memory_space=pl.ANY)],
        out_specs=vmem,
        scratch_shapes=[
            pltpu.VMEM((Z * RT, SZ * T), BF16),
            pltpu.VMEM((SZ * T, Z * RT), BF16),
            pltpu.VMEM((2, PATCHES, X * PATCHES), BF16),
            pltpu.VMEM((S, PATCHES, C), BF16),
            pltpu.VMEM((NC, SZ, W, C), BF16),
            pltpu.VMEM((2, NC, 4, R, W, C), BF16),
            pltpu.VMEM((2, NC, 4, R, W, C), BF16),
            pltpu.VMEM((NC, R, W, C), BF16),
            pltpu.VMEM((X, 2, PATCHES, C), BF16),
            pltpu.VMEM((PATCHES, 2 * C), F32),
            pltpu.VMEM((2, PATCHES, C), BF16),
            pltpu.VMEM((NC, Z, R, W, C), BF16),
            pltpu.VMEM((NC, SZ, W, C), BF16),
            pltpu.VMEM((S, PATCHES, C), BF16),
            dma,
            dma((NC, Q)), dma((NC, Q)),
            dma((2, NC, 4)), dma((2, NC, 4)),
            dma((NC, Q)), dma((NC, Q)),
            dma((2, 2, NC)), dma((2, 2, NC)),
            dma((NC, Q)), dma((NC, Q)),
            dma((2, NC, 4)), dma((2, NC, 4)),
            dma((NC, Q)), dma((NC, Q)),
        ],
        compiler_params=pltpu.CompilerParams(
            collective_id=0, has_side_effects=True, vmem_limit_bytes=56 * 2**20
        ),
    )(emissive, emission, ftab, itab, view_factor[0])


def solution(mesh):
    placed = (P("mode", "blk", None), P("blk"), P(), P(), P("mode", None, "blk", None))
    return jax.shard_map(
        local, mesh=mesh, in_specs=placed, out_specs=P("mode", "blk", None), check_vma=False
    )
```

```python
import functools
import math

import jax
import jax.numpy as jnp
from jax import lax
from jax.experimental import pallas as pl
from jax.experimental.pallas import tpu as pltpu
from jax.sharding import PartitionSpec as P

A = 512
Z, Y, CORES, X = 8, 4, 2, 4
Q = Y * CORES
S = A // (Z * Q)
SZ = S * Q
T = 16
L = 64
HALVES = ((16, 32), (16, 16, 16))
CHUNKS = tuple((h, sum(ws[:n]), w) for h, ws in enumerate(HALVES) for n, w in enumerate(ws))
NC = len(CHUNKS)
FIRST = tuple(n for n, c in enumerate(CHUNKS) if c[1] == 0)
LAST = tuple(n - 1 for n in FIRST[1:] + (NC,))
W = sum(HALVES[0])
PAIRS = W * Q
PATCHES = 2 * PAIRS
C = 128
R = 2 * Q
RT = R * T
MODES = Z * Q
MESH = pl.DeviceIdType.MESH
F32, BF16 = jnp.float32, jnp.bfloat16
HIGHEST = lax.Precision.HIGHEST
ORDER = (
    0, 1, 0, 3, 4, 0, 1, 0, 1, 4, 0, 1, 2, 1, 0, 2, 4, 1, 3, 0, 2, 4, 0, 3, 1, 2, 4, 0, 3, 1,
    3, 1, 2, 3, 4, 0, 2, 1, 3, 4, 2, 0, 1, 3, 4, 2, 0, 3, 1, 2, 4, 0, 1, 2, 4, 3, 1, 2, 4, 3,
    0, 2, 4, 2, 4, 3, 2, 3, 4, 0, 3, 1, 2, 4, 3,
)


def iota(shape, axis):
    return lax.broadcasted_iota(jnp.int32, shape, axis)


def flag(where):
    return jnp.where(where, 1.0, 0.0)


def swap(value):
    return pltpu.roll(value, L, 1)


def pack(left, right):
    return jnp.where(iota(left.shape, 1) < L, left, right)


def spread(table_ref, out_ref):
    rows, width = table_ref.shape
    mask = iota((T, width), 0) == iota((T, width), 1) % T

    def body(b, _):
        block = table_ref[pl.ds(pl.multiple_of(b * 8, 8), 8), :]
        for i in range(8):
            row = jnp.broadcast_to(block[i : i + 1, :], (T, width))
            at = pl.multiple_of((b * 8 + i) * T, T)
            out_ref[pl.ds(at, T), :] = jnp.where(mask, row, 0.0).astype(BF16)
        return 0

    lax.fori_loop(0, rows // 8, body, 0)


def kernel(
    emissive, classes, emissivity, mode_ids, factor_hbm, out,
    emission, ftab, itab, fk, ik, factor, emitted, station, rs_out, rs_in, spec, xs, acc, refl,
    gath, irr_out, irr,
    f_sem, a_send, a_recv, rs_send, rs_recv, c_send, c_recv, x_send, x_recv,
    d_send, d_recv, g_send, g_recv, h_send, h_recv,
):
    me, x = lax.axis_index("mode"), lax.axis_index("blk")
    z, q = me // Q, me % Q
    y, core = q // CORES, q % CORES

    def at_q(other):
        return {"mode": z * Q + other, "blk": x}

    def at_z(step):
        return {"mode": ((z + step + Z) % Z) * Q + q, "blk": x}

    def at_x(step):
        return {"mode": me, "blk": (x + step + X) % X}

    def copy(src, dst, send, recv, device):
        return pltpu.make_async_remote_copy(
            src_ref=src, dst_ref=dst, send_sem=send, recv_sem=recv,
            device_id=device, device_id_type=MESH,
        )

    sent = []
    begun = []

    def send(src, dst, s, r, device):
        op = copy(src, dst, s, r, device)
        op.start()
        sent.append(op)

    def arrived(dst, s, r):
        copy(dst, dst, s, r, at_z(1)).wait_recv()

    load = pltpu.make_async_copy(factor_hbm, factor, f_sem)
    load.start()

    barrier = pltpu.get_barrier_semaphore()
    peers = [at_q((q + k) % Q) for k in range(1, Q)]
    peers += [at_z(1), at_z(-1), at_x(1), at_x(-1)]
    for device in peers:
        pl.semaphore_signal(barrier, inc=1, device_id=device, device_id_type=MESH)

    def cols(c):
        h, at, w = CHUNKS[c]
        return pl.ds(h * W + at, w)

    def rows(c, bottom=0):
        _, at, w = CHUNKS[c]
        return pl.ds(at * Q + bottom * PAIRS, w * Q)

    def rows_of(c, other):
        _, at, w = CHUNKS[c]
        return pl.ds(pl.multiple_of(at * Q + other * w, T), w)

    def tiles(c):
        h, at, w = CHUNKS[c]
        return [slice(h * W + at + t, h * W + at + t + T) for t in range(0, w, T)]

    def absorb():
        rates = jnp.dot(
            emissivity[...], flag(iota((Q, C), 1) % Q == iota((Q, C), 0)),
            precision=HIGHEST, preferred_element_type=F32,
        )
        pick = flag(iota((Q, PATCHES), 0) == jnp.broadcast_to(classes[...], (Q, PATCHES)))
        value = lax.dot_general(
            pick, rates, (((0,), (0,)), ((), ())), precision=HIGHEST, preferred_element_type=F32
        )
        emission[...] = pack(value[:PAIRS], value[PAIRS:])

    def transforms():
        ids = jnp.broadcast_to(mode_ids[...], (8, MODES)).astype(F32).astype(BF16)
        twin = flag(iota((MODES, 2 * MODES), 1) // 2 == iota((MODES, 2 * MODES), 0)).astype(BF16)
        ids = jnp.dot(ids, twin, preferred_element_type=F32)[0:1, :]
        shape = (SZ, 2 * MODES)
        stations = (iota(shape, 0) + z * SZ).astype(F32)
        quarter = (iota(shape, 1) % 2 * (A // 4)).astype(F32)
        twists = ids * stations + quarter
        twists = twists - A * jnp.floor(twists * (1.0 / A))
        waves = jnp.cos(twists * (2.0 * math.pi / A))
        weight = jnp.where((ids == 0) | (ids == A // 2), 1.0 / A, 2.0 / A)
        forward = waves.T.astype(BF16)
        inverse = (weight * waves).astype(BF16)
        repeat = flag(iota((SZ, SZ * T), 1) // T == iota((SZ, SZ * T), 0)).astype(BF16)
        ftab[...] = jnp.dot(forward, repeat, preferred_element_type=F32)
        repeat = flag(iota((Z * R, Z * RT), 1) // T == iota((Z * R, Z * RT), 0)).astype(BF16)
        itab[...] = jnp.dot(inverse, repeat, preferred_element_type=F32)
        spread(ftab, fk)
        spread(itab, ik)

    def emit(c):
        h = CHUNKS[c][0]
        share = emission[rows(c), :]

        def body(s, _):
            top = emissive[s, rows(c), :].astype(F32)
            bottom = emissive[s, rows(c, 1), :].astype(F32)
            value = pack(top, swap(bottom)) if h == 0 else pack(swap(top), bottom)
            emitted[h, s, rows(c), :] = (share * value).astype(BF16)
            return 0

        lax.fori_loop(0, S, body, 0)

    def stations_out(c):
        for k in range(1, Q):
            other = (q + k) % Q
            send(
                emitted.at[CHUNKS[c][0], :, rows_of(c, other), :], station.at[pl.ds(q * S, S), cols(c), :],
                a_send.at[c, k], a_recv.at[c, k], at_q(other),
            )
        station[pl.ds(q * S, S), cols(c), :] = emitted[CHUNKS[c][0], :, rows_of(c, q), :]

    def stations_in(c):
        for k in range(1, Q):
            other = (q - k + Q) % Q
            arrived(
                station.at[pl.ds(other * S, S), cols(c), :], a_send.at[c, k], a_recv.at[c, k]
            )

    def wide(parts):
        return parts[0] if len(parts) == 1 else jnp.concatenate(parts, axis=1)

    def partial(c, target):
        right = wide([station[:, t, :].reshape(SZ * T, C) for t in tiles(c)])
        left = fk[pl.ds(pl.multiple_of(target * RT, RT), RT), :]
        value = jnp.dot(left, right, preferred_element_type=F32)
        return [
            (t, value[:, g * C : (g + 1) * C].reshape(R, T, C)) for g, t in enumerate(tiles(c))
        ]

    half = R // 2

    def rs_step(c, t):
        if t == 0:
            stations_in(c)
            value = partial(c, (z + 4) % Z)
            for way in range(2):
                hit = slice(way * half, (way + 1) * half)
                for at, mine in value:
                    rs_out[way, 0, hit, at, :] = mine[hit].astype(BF16)
                block = (way, 0, pl.ds(way * half, half), cols(c))
                send(
                    rs_out.at[block], rs_in.at[block],
                    rs_send.at[way, c, 0], rs_recv.at[way, c, 0], at_z(1 - 2 * way),
                )
            return
        for way in range(2):
            value = partial(c, (z + 4 - t) % Z if way == 0 else (z + 4 + t) % Z)
            hit = slice(way * half, (way + 1) * half) if t == 1 else slice(0, R)
            miss = slice((1 - way) * half, (2 - way) * half)
            block = (way, t - 1, pl.ds(hit.start, hit.stop - hit.start), cols(c))
            arrived(rs_in.at[block], rs_send.at[way, c, t - 1], rs_recv.at[way, c, t - 1])
            for at, mine in value:
                total = mine[hit] + rs_in[way, t - 1, hit, at, :].astype(F32)
                rs_out[way, t, hit, at, :] = total.astype(BF16)
                if t == 1:
                    rs_out[way, t, miss, at, :] = mine[miss].astype(BF16)
            block = (way, t, slice(None), cols(c))
            send(
                rs_out.at[block], rs_in.at[block],
                rs_send.at[way, c, t], rs_recv.at[way, c, t], at_z(1 - 2 * way),
            )

    def rs_final(c):
        value = partial(c, z)
        for way in range(2):
            block = (way, 3, slice(None), cols(c))
            arrived(rs_in.at[block], rs_send.at[way, c, 3], rs_recv.at[way, c, 3])
        for at, mine in value:
            total = mine + (rs_in[0, 3, :, at, :].astype(F32) + rs_in[1, 3, :, at, :].astype(F32))
            spec[:, at, :] = total.astype(BF16)
        for k in range(1, Q):
            other = (q + k) % Q
            send(
                spec.at[pl.ds(other * 2, 2), cols(c), :], xs.at[CHUNKS[c][0], x, :, rows_of(c, q), :],
                c_send.at[c, k], c_recv.at[c, k], at_q(other),
            )
        xs[CHUNKS[c][0], x, :, rows_of(c, q), :] = spec[pl.ds(q * 2, 2), cols(c), :]

    def gather_first(c):
        for k in range(1, Q):
            other = (q - k + Q) % Q
            arrived(xs.at[CHUNKS[c][0], x, :, rows_of(c, other), :], c_send.at[c, k], c_recv.at[c, k])
        for way in range(2):
            block = xs.at[CHUNKS[c][0], x, :, rows(c), :]
            send(block, block, x_send.at[0, way, c], x_recv.at[0, way, c], at_x(1 - 2 * way))

    def spectrum(c, sources):
        parts = []
        for source in sources:
            real = xs[CHUNKS[c][0], source, 0, rows(c), :].astype(F32)
            imag = xs[CHUNKS[c][0], source, 1, rows(c), :].astype(F32)
            parts += [pack(real, swap(imag)), pack(-imag, swap(real))]
            parts += [pack(swap(real), imag), pack(-swap(imag), real)]
        return jnp.concatenate([part.astype(BF16) for part in parts], axis=0)

    def factors(c, sources, to):
        _, first, w = CHUNKS[c]
        parts = []
        for source in sources:
            for bottom in range(2):
                at = source * PATCHES + bottom * PAIRS + first * Q
                if not isinstance(source, int):
                    at = pl.multiple_of(at, C)
                parts += [factor[part, to, pl.ds(at, w * Q)] for part in range(2)]
        return wide(parts)

    def reflect(c, sources):
        h = CHUNKS[c][0]
        fresh = h not in begun
        begun.append(h)
        right = spectrum(c, sources)

        def body(b, _):
            to = pl.ds(pl.multiple_of(b * 256, 256), 256)
            value = jnp.dot(factors(c, sources, to), right, preferred_element_type=F32)
            acc[h, to, :] = value if fresh else acc[h, to, :] + value
            return 0

        lax.fori_loop(0, PATCHES // 256, body, 0)

    def gather_second(c):
        sides = [(x + X - 1) % X, (x + 1) % X]
        for way, source in enumerate(sides):
            block = xs.at[CHUNKS[c][0], source, :, rows(c), :]
            arrived(block, x_send.at[0, way, c], x_recv.at[0, way, c])
            block = xs.at[CHUNKS[c][0], source, way, rows(c), :]
            send(block, block, x_send.at[1, way, c], x_recv.at[1, way, c], at_x(1 - 2 * way))
        if c == 0:
            load.wait()
        if c in LAST:
            reflect(c, [x] + sides)

    def gather_third(c):
        source = (x + 2) % X
        for way in range(2):
            block = xs.at[CHUNKS[c][0], source, way, rows(c), :]
            arrived(block, x_send.at[1, way, c], x_recv.at[1, way, c])
        if c not in LAST:
            reflect(c, range(X))
            return
        h = CHUNKS[c][0]
        right = spectrum(c, [source])
        for b in range(FIRST[h], c + 1):
            both = []
            for bottom in range(2):
                to = rows(b, bottom)
                value = jnp.dot(factors(c, [source], to), right, preferred_element_type=F32)
                both.append(acc[h, to, :] + value)
            top, bottom = both
            refl[h, 0, rows(b), :] = pack(top, swap(bottom)).astype(BF16)
            refl[h, 1, rows(b), :] = pack(swap(top), bottom).astype(BF16)
            for k in range(1, Q):
                other = (q + k) % Q
                send(
                    refl.at[h, :, rows_of(b, other), :], gath.at[z, pl.ds(q * 2, 2), cols(b), :],
                    d_send.at[b, k], d_recv.at[b, k], at_q(other),
                )
            gath[z, pl.ds(q * 2, 2), cols(b), :] = refl[h, :, rows_of(b, q), :]

    def ag_step(c, t):
        if t == 0:
            for k in range(1, Q):
                other = (q - k + Q) % Q
                arrived(
                    gath.at[z, pl.ds(other * 2, 2), cols(c), :], d_send.at[c, k], d_recv.at[c, k]
                )
        for way in range(2):
            source = (z - t + Z) % Z if way == 0 else (z + t) % Z
            block = gath.at[source, :, cols(c), :]
            if t > 0:
                arrived(block, g_send.at[way, c, t - 1], g_recv.at[way, c, t - 1])
            if t == 3:
                block = gath.at[source, pl.ds(way * half, half), cols(c), :]
            send(block, block, g_send.at[way, c, t], g_recv.at[way, c, t], at_z(1 - 2 * way))

    def irradiance_out(c):
        for way in range(2):
            block = gath.at[(z + 4) % Z, pl.ds(way * half, half), cols(c), :]
            arrived(block, g_send.at[way, c, 3], g_recv.at[way, c, 3])
        right = wide([gath[:, :, t, :].reshape(Z * RT, C) for t in tiles(c)])
        count = 2 * S * T
        for k in range(Y):
            other = (y + k) % Y
            left = ik[pl.ds(pl.multiple_of(other * count, count), count), :]
            value = jnp.dot(left, right, preferred_element_type=F32).astype(BF16)
            for g, t in enumerate(tiles(c)):
                irr_out[pl.ds(other * 2 * S, 2 * S), t, :] = (
                    value[:, g * C : (g + 1) * C].reshape(2 * S, T, C)
                )
            for j in range(CORES):
                if k == 0 and j == 0:
                    continue
                to = other * CORES + (core + j) % CORES
                n = k * CORES + j
                send(
                    irr_out.at[pl.ds(to * S, S), cols(c), :], irr.at[CHUNKS[c][0], :, rows_of(c, q), :],
                    h_send.at[c, n], h_recv.at[c, n], at_q(to),
                )
        irr[CHUNKS[c][0], :, rows_of(c, q), :] = irr_out[pl.ds(q * S, S), cols(c), :]

    def finish(c):
        for k in range(Y):
            for j in range(CORES):
                if k == 0 and j == 0:
                    continue
                source = ((y - k + Y) % Y) * CORES + (core + j) % CORES
                n = k * CORES + j
                arrived(irr.at[CHUNKS[c][0], :, rows_of(c, source), :], h_send.at[c, n], h_recv.at[c, n])
        h = CHUNKS[c][0]
        rest = 1.0 - emission[rows(c), :]

        def body(s, _):
            value = irr[h, s, rows(c), :].astype(F32)
            value = emitted[h, s, rows(c), :].astype(F32) + rest * value
            if h == 0:
                irr[0, s, rows(c), :] = value.astype(BF16)
            else:
                other = irr[0, s, rows(c), :].astype(F32)
                out[s, rows(c), :] = pack(other, swap(value)).astype(BF16)
                out[s, rows(c, 1), :] = pack(swap(other), value).astype(BF16)
            return 0

        lax.fori_loop(0, S, body, 0)

    def start(c):
        emit(c)
        stations_out(c)

    absorb()
    pl.semaphore_wait(barrier, len(peers))
    stages = [start] + [functools.partial(rs_step, t=t) for t in range(4)]
    stages += [rs_final, gather_first, gather_second, gather_third]
    stages += [functools.partial(ag_step, t=t) for t in range(4)] + [irradiance_out, finish]
    done = [0] * NC
    ready = False
    for c in ORDER:
        if done[c] == 1 and not ready:
            transforms()
            ready = True
        stages[done[c]](c)
        done[c] += 1
    for op in sent:
        op.wait_send()


def local(emissive, classes, emissivity, mode_ids, view_factor):
    vmem = pl.BlockSpec(memory_space=pltpu.VMEM)
    dma = pltpu.SemaphoreType.DMA
    return pl.pallas_call(
        kernel,
        out_shape=jax.ShapeDtypeStruct(emissive.shape, BF16),
        in_specs=[vmem] * 4 + [pl.BlockSpec(memory_space=pl.ANY)],
        out_specs=vmem,
        scratch_shapes=[
            pltpu.VMEM((PAIRS, C), F32),
            pltpu.VMEM((Z * R, SZ * T), F32),
            pltpu.VMEM((SZ, Z * RT), F32),
            pltpu.VMEM((Z * RT, SZ * T), BF16),
            pltpu.VMEM((SZ * T, Z * RT), BF16),
            pltpu.VMEM((2, PATCHES, X * PATCHES), BF16),
            pltpu.VMEM((2, S, PAIRS, C), BF16),
            pltpu.VMEM((SZ, 2 * W, C), BF16),
            pltpu.VMEM((2, 4, R, 2 * W, C), BF16),
            pltpu.VMEM((2, 4, R, 2 * W, C), BF16),
            pltpu.VMEM((R, 2 * W, C), BF16),
            pltpu.VMEM((2, X, 2, PAIRS, C), BF16),
            pltpu.VMEM((2, PATCHES, C), F32),
            pltpu.VMEM((2, 2, PAIRS, C), BF16),
            pltpu.VMEM((Z, R, 2 * W, C), BF16),
            pltpu.VMEM((SZ, 2 * W, C), BF16),
            pltpu.VMEM((2, S, PAIRS, C), BF16),
            dma,
            dma((NC, Q)), dma((NC, Q)),
            dma((2, NC, 4)), dma((2, NC, 4)),
            dma((NC, Q)), dma((NC, Q)),
            dma((2, 2, NC)), dma((2, 2, NC)),
            dma((NC, Q)), dma((NC, Q)),
            dma((2, NC, 4)), dma((2, NC, 4)),
            dma((NC, Q)), dma((NC, Q)),
        ],
        compiler_params=pltpu.CompilerParams(
            collective_id=0, has_side_effects=True, vmem_limit_bytes=56 * 2**20
        ),
    )(emissive, classes[None, :], emissivity, mode_ids[None, :], view_factor[0])


def solution(mesh):
    placed = (P("mode", "blk", None), P("blk"), P(), P(), P("mode", None, "blk", None))
    return jax.shard_map(
        local, mesh=mesh, in_specs=placed, out_specs=P("mode", "blk", None), check_vma=False
    )
```

```python
import functools
import math

import jax
import jax.numpy as jnp
from jax import lax
from jax.experimental import pallas as pl
from jax.experimental.pallas import tpu as pltpu
from jax.sharding import PartitionSpec as P

A = 512
Z, Y, CORES, X = 8, 4, 2, 4
Q = Y * CORES
S = A // (Z * Q)
SZ = S * Q
T = 16
L = 64
HALVES = ((16, 32), (16, 32))
CHUNKS = tuple((h, sum(ws[:n]), w) for h, ws in enumerate(HALVES) for n, w in enumerate(ws))
NC = len(CHUNKS)
FIRST = tuple(n for n, c in enumerate(CHUNKS) if c[1] == 0)
LAST = tuple(n - 1 for n in FIRST[1:] + (NC,))
W = sum(HALVES[0])
PAIRS = W * Q
PATCHES = 2 * PAIRS
C = 128
R = 2 * Q
RT = R * T
MODES = Z * Q
MESH = pl.DeviceIdType.MESH
F32, BF16 = jnp.float32, jnp.bfloat16
HIGHEST = lax.Precision.HIGHEST
ORDER = (
    0, 1, 0, 2, 0, 1, 3, 0, 1, 0, 2, 1, 0, 3, 2, 0, 1, 0, 3, 1, 2, 3, 0, 2, 1, 3, 1, 2, 1, 3,
    2, 0, 2, 0, 3, 1, 2, 0, 3, 1, 3, 0, 1, 2, 3, 2, 0, 1, 3, 1, 2, 3, 2, 3, 2, 0, 3, 1, 2, 3,
)


def iota(shape, axis):
    return lax.broadcasted_iota(jnp.int32, shape, axis)


def flag(where):
    return jnp.where(where, 1.0, 0.0)


def swap(value):
    return pltpu.roll(value, L, 1)


def pack(left, right):
    return jnp.where(iota(left.shape, 1) < L, left, right)


def spread(table_ref, out_ref):
    rows, width = table_ref.shape
    mask = iota((T, width), 0) == iota((T, width), 1) % T

    def body(b, _):
        block = table_ref[pl.ds(pl.multiple_of(b * 8, 8), 8), :]
        for i in range(8):
            row = jnp.broadcast_to(block[i : i + 1, :], (T, width))
            at = pl.multiple_of((b * 8 + i) * T, T)
            out_ref[pl.ds(at, T), :] = jnp.where(mask, row, 0.0).astype(BF16)
        return 0

    lax.fori_loop(0, rows // 8, body, 0)


def kernel(
    emissive, classes, emissivity, mode_ids, factor_hbm, out,
    emission, ftab, itab, fk, ik, factor, emitted, station, terms, rs_out, rs_in, spec, xs, acc, refl,
    gath, irr_out, irr,
    f_sem, a_send, a_recv, rs_send, rs_recv, c_send, c_recv, x_send, x_recv,
    d_send, d_recv, g_send, g_recv, h_send, h_recv,
):
    me, x = lax.axis_index("mode"), lax.axis_index("blk")
    z, q = me // Q, me % Q
    y, core = q // CORES, q % CORES

    def at_q(other):
        return {"mode": z * Q + other, "blk": x}

    def at_z(step):
        return {"mode": ((z + step + Z) % Z) * Q + q, "blk": x}

    def at_x(step):
        return {"mode": me, "blk": (x + step + X) % X}

    def copy(src, dst, send, recv, device):
        return pltpu.make_async_remote_copy(
            src_ref=src, dst_ref=dst, send_sem=send, recv_sem=recv,
            device_id=device, device_id_type=MESH,
        )

    sent = []
    begun = []

    def send(src, dst, s, r, device):
        op = copy(src, dst, s, r, device)
        op.start()
        sent.append(op)

    def arrived(dst, s, r):
        copy(dst, dst, s, r, at_z(1)).wait_recv()

    load = pltpu.make_async_copy(factor_hbm, factor, f_sem)
    load.start()

    barrier = pltpu.get_barrier_semaphore()
    peers = [at_q((q + k) % Q) for k in range(1, Q)]
    peers += [at_z(1), at_z(-1), at_x(1), at_x(-1)]
    for device in peers:
        pl.semaphore_signal(barrier, inc=1, device_id=device, device_id_type=MESH)

    def cols(c):
        h, at, w = CHUNKS[c]
        return pl.ds(h * W + at, w)

    def rows(c, bottom=0):
        _, at, w = CHUNKS[c]
        return pl.ds(at * Q + bottom * PAIRS, w * Q)

    def rows_of(c, other):
        _, at, w = CHUNKS[c]
        return pl.ds(pl.multiple_of(at * Q + other * w, T), w)

    def tiles(c):
        h, at, w = CHUNKS[c]
        return [slice(h * W + at + t, h * W + at + t + T) for t in range(0, w, T)]

    def absorb():
        rates = jnp.dot(
            emissivity[...], flag(iota((Q, C), 1) % Q == iota((Q, C), 0)),
            precision=HIGHEST, preferred_element_type=F32,
        )
        pick = flag(iota((Q, PATCHES), 0) == jnp.broadcast_to(classes[...], (Q, PATCHES)))
        value = lax.dot_general(
            pick, rates, (((0,), (0,)), ((), ())), precision=HIGHEST, preferred_element_type=F32
        )
        emission[...] = pack(value[:PAIRS], value[PAIRS:])

    def transforms():
        ids = jnp.broadcast_to(mode_ids[...], (8, MODES)).astype(F32).astype(BF16)
        twin = flag(iota((MODES, 2 * MODES), 1) // 2 == iota((MODES, 2 * MODES), 0)).astype(BF16)
        ids = jnp.dot(ids, twin, preferred_element_type=F32)[0:1, :]
        shape = (SZ, 2 * MODES)
        stations = (iota(shape, 0) + z * SZ).astype(F32)
        quarter = (iota(shape, 1) % 2 * (A // 4)).astype(F32)
        twists = ids * stations + quarter
        twists = twists - A * jnp.floor(twists * (1.0 / A))
        waves = jnp.cos(twists * (2.0 * math.pi / A))
        weight = jnp.where((ids == 0) | (ids == A // 2), 1.0 / A, 2.0 / A)
        forward = waves.T.astype(BF16)
        inverse = (weight * waves).astype(BF16)
        repeat = flag(iota((SZ, SZ * T), 1) // T == iota((SZ, SZ * T), 0)).astype(BF16)
        ftab[...] = jnp.dot(forward, repeat, preferred_element_type=F32)
        repeat = flag(iota((Z * R, Z * RT), 1) // T == iota((Z * R, Z * RT), 0)).astype(BF16)
        itab[...] = jnp.dot(inverse, repeat, preferred_element_type=F32)
        spread(ftab, fk)
        spread(itab, ik)

    def emit(c):
        h = CHUNKS[c][0]
        share = emission[rows(c), :]

        def body(s, _):
            top = emissive[s, rows(c), :].astype(F32)
            bottom = emissive[s, rows(c, 1), :].astype(F32)
            value = pack(top, swap(bottom)) if h == 0 else pack(swap(top), bottom)
            emitted[h, s, rows(c), :] = (share * value).astype(BF16)
            return 0

        lax.fori_loop(0, S, body, 0)

    def stations_out(c):
        for k in range(1, Q):
            other = (q + k) % Q
            send(
                emitted.at[CHUNKS[c][0], :, rows_of(c, other), :], station.at[pl.ds(q * S, S), cols(c), :],
                a_send.at[c, k], a_recv.at[c, k], at_q(other),
            )
        station[pl.ds(q * S, S), cols(c), :] = emitted[CHUNKS[c][0], :, rows_of(c, q), :]

    def stations_in(c):
        for k in range(1, Q):
            other = (q - k + Q) % Q
            arrived(
                station.at[pl.ds(other * S, S), cols(c), :], a_send.at[c, k], a_recv.at[c, k]
            )

    def wide(parts):
        return parts[0] if len(parts) == 1 else jnp.concatenate(parts, axis=1)

    def partial(c, left):
        right = wide([station[:, t, :].reshape(SZ * T, C) for t in tiles(c)])
        value = jnp.dot(left, right, preferred_element_type=F32)
        return [
            (t, value[:, g * C : (g + 1) * C].reshape(-1, R, T, C)) for g, t in enumerate(tiles(c))
        ]

    def partials(c):
        def body(b, _):
            left = fk[pl.ds(pl.multiple_of(b * 2 * RT, 2 * RT), 2 * RT), :]
            for t, value in partial(c, left):
                terms[pl.ds(b * 2, 2), :, t, :] = value
            return 0

        lax.fori_loop(0, Z // 2, body, 0)

    half = R // 2

    def rs_step(c, t):
        if t == 0:
            stations_in(c)
            far = (z + 4) % Z
            value = partial(c, fk[pl.ds(pl.multiple_of(far * RT, RT), RT), :])
            for way in range(2):
                hit = slice(way * half, (way + 1) * half)
                for at, mine in value:
                    rs_out[way, 0, hit, at, :] = mine[0, hit].astype(BF16)
                block = (way, 0, pl.ds(way * half, half), cols(c))
                send(
                    rs_out.at[block], rs_in.at[block],
                    rs_send.at[way, c, 0], rs_recv.at[way, c, 0], at_z(1 - 2 * way),
                )
            partials(c)
            return
        for way in range(2):
            target = (z + 4 - t) % Z if way == 0 else (z + 4 + t) % Z
            hit = slice(way * half, (way + 1) * half) if t == 1 else slice(0, R)
            miss = slice((1 - way) * half, (2 - way) * half)
            block = (way, t - 1, pl.ds(hit.start, hit.stop - hit.start), cols(c))
            arrived(rs_in.at[block], rs_send.at[way, c, t - 1], rs_recv.at[way, c, t - 1])
            for at in tiles(c):
                total = terms[target, hit, at, :] + rs_in[way, t - 1, hit, at, :].astype(F32)
                rs_out[way, t, hit, at, :] = total.astype(BF16)
                if t == 1:
                    rs_out[way, t, miss, at, :] = terms[target, miss, at, :].astype(BF16)
            block = (way, t, slice(None), cols(c))
            send(
                rs_out.at[block], rs_in.at[block],
                rs_send.at[way, c, t], rs_recv.at[way, c, t], at_z(1 - 2 * way),
            )

    def rs_final(c):
        for way in range(2):
            block = (way, 3, slice(None), cols(c))
            arrived(rs_in.at[block], rs_send.at[way, c, 3], rs_recv.at[way, c, 3])
        for at in tiles(c):
            total = terms[z, :, at, :] + (rs_in[0, 3, :, at, :].astype(F32) + rs_in[1, 3, :, at, :].astype(F32))
            spec[:, at, :] = total.astype(BF16)
        for k in range(1, Q):
            other = (q + k) % Q
            send(
                spec.at[pl.ds(other * 2, 2), cols(c), :], xs.at[CHUNKS[c][0], x, :, rows_of(c, q), :],
                c_send.at[c, k], c_recv.at[c, k], at_q(other),
            )
        xs[CHUNKS[c][0], x, :, rows_of(c, q), :] = spec[pl.ds(q * 2, 2), cols(c), :]

    def gather_first(c):
        for k in range(1, Q):
            other = (q - k + Q) % Q
            arrived(xs.at[CHUNKS[c][0], x, :, rows_of(c, other), :], c_send.at[c, k], c_recv.at[c, k])
        for way in range(2):
            block = xs.at[CHUNKS[c][0], x, :, rows(c), :]
            send(block, block, x_send.at[0, way, c], x_recv.at[0, way, c], at_x(1 - 2 * way))

    def spectrum(c, sources):
        parts = []
        for source in sources:
            real = xs[CHUNKS[c][0], source, 0, rows(c), :].astype(F32)
            imag = xs[CHUNKS[c][0], source, 1, rows(c), :].astype(F32)
            parts += [pack(real, swap(imag)), pack(-imag, swap(real))]
            parts += [pack(swap(real), imag), pack(-swap(imag), real)]
        return jnp.concatenate([part.astype(BF16) for part in parts], axis=0)

    def factors(c, sources, to):
        _, first, w = CHUNKS[c]
        parts = []
        for source in sources:
            for bottom in range(2):
                at = source * PATCHES + bottom * PAIRS + first * Q
                if not isinstance(source, int):
                    at = pl.multiple_of(at, C)
                parts += [factor[part, to, pl.ds(at, w * Q)] for part in range(2)]
        return wide(parts)

    def reflect(c, sources):
        h = CHUNKS[c][0]
        fresh = h not in begun
        begun.append(h)
        right = spectrum(c, sources)

        def body(b, _):
            to = pl.ds(pl.multiple_of(b * 256, 256), 256)
            value = jnp.dot(factors(c, sources, to), right, preferred_element_type=F32)
            acc[h, to, :] = value if fresh else acc[h, to, :] + value
            return 0

        lax.fori_loop(0, PATCHES // 256, body, 0)

    def gather_second(c):
        sides = [(x + X - 1) % X, (x + 1) % X]
        for way, source in enumerate(sides):
            block = xs.at[CHUNKS[c][0], source, :, rows(c), :]
            arrived(block, x_send.at[0, way, c], x_recv.at[0, way, c])
            block = xs.at[CHUNKS[c][0], source, way, rows(c), :]
            send(block, block, x_send.at[1, way, c], x_recv.at[1, way, c], at_x(1 - 2 * way))
        if c == 0:
            load.wait()
        if c in LAST:
            reflect(c, [x] + sides)

    def gather_third(c):
        source = (x + 2) % X
        for way in range(2):
            block = xs.at[CHUNKS[c][0], source, way, rows(c), :]
            arrived(block, x_send.at[1, way, c], x_recv.at[1, way, c])
        if c not in LAST:
            reflect(c, range(X))
            return
        h = CHUNKS[c][0]
        right = spectrum(c, [source])
        for b in range(FIRST[h], c + 1):
            both = []
            for bottom in range(2):
                to = rows(b, bottom)
                value = jnp.dot(factors(c, [source], to), right, preferred_element_type=F32)
                both.append(acc[h, to, :] + value)
            top, bottom = both
            refl[h, 0, rows(b), :] = pack(top, swap(bottom)).astype(BF16)
            refl[h, 1, rows(b), :] = pack(swap(top), bottom).astype(BF16)
            for k in range(1, Q):
                other = (q + k) % Q
                send(
                    refl.at[h, :, rows_of(b, other), :], gath.at[z, pl.ds(q * 2, 2), cols(b), :],
                    d_send.at[b, k], d_recv.at[b, k], at_q(other),
                )
            gath[z, pl.ds(q * 2, 2), cols(b), :] = refl[h, :, rows_of(b, q), :]

    def ag_step(c, t):
        if t == 0:
            for k in range(1, Q):
                other = (q - k + Q) % Q
                arrived(
                    gath.at[z, pl.ds(other * 2, 2), cols(c), :], d_send.at[c, k], d_recv.at[c, k]
                )
        for way in range(2):
            source = (z - t + Z) % Z if way == 0 else (z + t) % Z
            block = gath.at[source, :, cols(c), :]
            if t > 0:
                arrived(block, g_send.at[way, c, t - 1], g_recv.at[way, c, t - 1])
            if t == 3:
                block = gath.at[source, pl.ds(way * half, half), cols(c), :]
            send(block, block, g_send.at[way, c, t], g_recv.at[way, c, t], at_z(1 - 2 * way))

    def irradiance_out(c):
        for way in range(2):
            block = gath.at[(z + 4) % Z, pl.ds(way * half, half), cols(c), :]
            arrived(block, g_send.at[way, c, 3], g_recv.at[way, c, 3])
        right = wide([gath[:, :, t, :].reshape(Z * RT, C) for t in tiles(c)])
        count = 2 * S * T
        for k in range(Y):
            other = (y + k) % Y
            left = ik[pl.ds(pl.multiple_of(other * count, count), count), :]
            value = jnp.dot(left, right, preferred_element_type=F32).astype(BF16)
            for g, t in enumerate(tiles(c)):
                irr_out[pl.ds(other * 2 * S, 2 * S), t, :] = (
                    value[:, g * C : (g + 1) * C].reshape(2 * S, T, C)
                )
            for j in range(CORES):
                if k == 0 and j == 0:
                    continue
                to = other * CORES + (core + j) % CORES
                n = k * CORES + j
                send(
                    irr_out.at[pl.ds(to * S, S), cols(c), :], irr.at[CHUNKS[c][0], :, rows_of(c, q), :],
                    h_send.at[c, n], h_recv.at[c, n], at_q(to),
                )
        irr[CHUNKS[c][0], :, rows_of(c, q), :] = irr_out[pl.ds(q * S, S), cols(c), :]

    def finish(c):
        for k in range(Y):
            for j in range(CORES):
                if k == 0 and j == 0:
                    continue
                source = ((y - k + Y) % Y) * CORES + (core + j) % CORES
                n = k * CORES + j
                arrived(irr.at[CHUNKS[c][0], :, rows_of(c, source), :], h_send.at[c, n], h_recv.at[c, n])
        h = CHUNKS[c][0]
        rest = 1.0 - emission[rows(c), :]

        def body(s, _):
            value = irr[h, s, rows(c), :].astype(F32)
            value = emitted[h, s, rows(c), :].astype(F32) + rest * value
            if h == 0:
                irr[0, s, rows(c), :] = value.astype(BF16)
            else:
                other = irr[0, s, rows(c), :].astype(F32)
                out[s, rows(c), :] = pack(other, swap(value)).astype(BF16)
                out[s, rows(c, 1), :] = pack(swap(other), value).astype(BF16)
            return 0

        lax.fori_loop(0, S, body, 0)

    def start(c):
        emit(c)
        stations_out(c)

    absorb()
    pl.semaphore_wait(barrier, len(peers))
    stages = [start] + [functools.partial(rs_step, t=t) for t in range(4)]
    stages += [rs_final, gather_first, gather_second, gather_third]
    stages += [functools.partial(ag_step, t=t) for t in range(4)] + [irradiance_out, finish]
    done = [0] * NC
    ready = False
    for c in ORDER:
        if done[c] == 1 and not ready:
            transforms()
            ready = True
        stages[done[c]](c)
        done[c] += 1
    for op in sent:
        op.wait_send()


def local(emissive, classes, emissivity, mode_ids, view_factor):
    vmem = pl.BlockSpec(memory_space=pltpu.VMEM)
    dma = pltpu.SemaphoreType.DMA
    return pl.pallas_call(
        kernel,
        out_shape=jax.ShapeDtypeStruct(emissive.shape, BF16),
        in_specs=[vmem] * 4 + [pl.BlockSpec(memory_space=pl.ANY)],
        out_specs=vmem,
        scratch_shapes=[
            pltpu.VMEM((PAIRS, C), F32),
            pltpu.VMEM((Z * R, SZ * T), F32),
            pltpu.VMEM((SZ, Z * RT), F32),
            pltpu.VMEM((Z * RT, SZ * T), BF16),
            pltpu.VMEM((SZ * T, Z * RT), BF16),
            pltpu.VMEM((2, PATCHES, X * PATCHES), BF16),
            pltpu.VMEM((2, S, PAIRS, C), BF16),
            pltpu.VMEM((SZ, 2 * W, C), BF16),
            pltpu.VMEM((Z, R, 2 * W, C), F32),
            pltpu.VMEM((2, 4, R, 2 * W, C), BF16),
            pltpu.VMEM((2, 4, R, 2 * W, C), BF16),
            pltpu.VMEM((R, 2 * W, C), BF16),
            pltpu.VMEM((2, X, 2, PAIRS, C), BF16),
            pltpu.VMEM((2, PATCHES, C), F32),
            pltpu.VMEM((2, 2, PAIRS, C), BF16),
            pltpu.VMEM((Z, R, 2 * W, C), BF16),
            pltpu.VMEM((SZ, 2 * W, C), BF16),
            pltpu.VMEM((2, S, PAIRS, C), BF16),
            dma,
            dma((NC, Q)), dma((NC, Q)),
            dma((2, NC, 4)), dma((2, NC, 4)),
            dma((NC, Q)), dma((NC, Q)),
            dma((2, 2, NC)), dma((2, 2, NC)),
            dma((NC, Q)), dma((NC, Q)),
            dma((2, NC, 4)), dma((2, NC, 4)),
            dma((NC, Q)), dma((NC, Q)),
        ],
        compiler_params=pltpu.CompilerParams(
            collective_id=0, has_side_effects=True, vmem_limit_bytes=50 * 2**20
        ),
    )(emissive, classes[None, :], emissivity, mode_ids[None, :], view_factor[0])


def solution(mesh):
    placed = (P("mode", "blk", None), P("blk"), P(), P(), P("mode", None, "blk", None))
    return jax.shard_map(
        local, mesh=mesh, in_specs=placed, out_specs=P("mode", "blk", None), check_vma=False
    )
```
